128 devices in a mesh: group: 4 (over x), member: 32 (over z, y, core).
Axes of the slice: x: 4, y: 4, z: 4, core: 2. Of those that a mesh axis runs over, the one named last changes fastest.
Arguments:
- mesh_vector: bfloat16 [131072, 128], P(('group', 'member')), may hold values from -6 to 6
- cluster_position: int32 [131072], P(('group', 'member')), may hold values from 0 to 131071, as said below
- cluster_sizes: int32 [128], replicated, may hold values from 256 to 1792, as said below
- block_ranks: int32 [254], replicated, may hold values from 32 to 128, as said below
- diag_block: bfloat16 [2, 229376, 1792], P(None, ('group', 'member')), may hold values from -0.09375 to 0.09375
- top_left: bfloat16 [2, 2, 229376, 128], P(None, None, ('group', 'member')), may hold values from -0.375 to 0.375
- top_right: bfloat16 [2, 2, 229376, 128], P(None, None, ('group', 'member'))
- low_left: bfloat16 [5, 2, 229376, 64], P(None, None, ('group', 'member')), may hold values from -0.5 to 0.5
- low_right: bfloat16 [5, 2, 229376, 64], P(None, None, ('group', 'member'))
Outputs:
- product: float32 [131072, 128], P(('group', 'member'))
The draws below stay inside these ranges and needn't reach their ends.
Inputs may be any that keep to these rules, and one draw needn't show every extreme that they name: `cluster_position`: A permutation of the unknowns. In cluster order every aligned run of 128 positions holds exactly one row of each device, so each device holds exactly size / 128 rows of every cluster. `cluster_sizes`: multiples of 128 that sum to 131072; one is exactly 1792. `block_ranks`: entries 0 .. 5 lie in 64 .. 128, the others in 32 .. 64; entry 0 is 128.
All inputs are finite; a program needn't handle non-finite values.
Results may differ from the reference program's by a relative error of at most 0.0027.
Values may be sent and summed in bfloat16 or wider, within the bound.
A program may use at most 64 MiB of HBM per device.

```python
import jax
import jax.numpy as jnp
from jax import lax

COLS = 128
R = 1024
K = 128
KM = 64
LEAVES = 128
NU = 131072
CAP = 1792
NS = 229376
GLEVELS = 2
MLEVELS = 5
TOPNODES = 6
HEAP = 254


def cluster_layout(key):
    layout_key = jax.random.fold_in(key, 101)
    average = R // LEAVES
    widest = (3 * average + 3) // 4
    pairs_count = LEAVES // 2
    pairing = jax.random.permutation(jax.random.fold_in(layout_key, 1), LEAVES)
    spread = jax.random.randint(jax.random.fold_in(layout_key, 2), (pairs_count,), 0, widest + 1)
    spread = spread.at[0].set(widest)
    paired_counts = jnp.concatenate([average + spread, average - spread]).astype(jnp.int32)
    counts = jnp.zeros((LEAVES,), jnp.int32).at[pairing].set(paired_counts)
    size_list = counts * LEAVES
    window_keys = jax.random.split(jax.random.fold_in(layout_key, 3), R)
    owners_of = jax.vmap(lambda one_key: jax.random.permutation(one_key, LEAVES))(window_keys)
    inverse = jnp.argsort(owners_of, axis=1).astype(jnp.int32)
    local_keys = jax.random.split(jax.random.fold_in(layout_key, 4), LEAVES)
    windows = jax.vmap(lambda one_key: jax.random.permutation(one_key, R))(local_keys).astype(jnp.int32)
    sources = jnp.arange(LEAVES, dtype=jnp.int32)[:, None]
    offsets = inverse[windows, sources]
    positions = windows * LEAVES + offsets
    return (size_list.astype(jnp.int32), positions.reshape(-1).astype(jnp.int32))


def draw_cluster_sizes(key, part):
    return cluster_layout(key)[0]


def draw_cluster_position(key, part):
    return cluster_layout(key)[1]


def draw_block_ranks(key, part):
    key = jax.random.fold_in(key, 7)
    positions_heap = jnp.arange(HEAP, dtype=jnp.int32)
    upper = positions_heap < TOPNODES
    lowest = jnp.where(upper, K // 2, KM // 2)
    highest = jnp.where(upper, K, KM)
    raw = jax.random.randint(key, (HEAP,), 0, 1 << 20)
    ranks = raw % (highest - lowest + 1) + lowest
    ranks = ranks.at[0].set(K)
    ranks = ranks.at[HEAP - 1].set(KM // 2)
    return ranks.astype(jnp.int32)


def factor_values(key, shape):
    return jax.random.normal(key, shape, jnp.float32)


def draw_top_right(key, part):
    key = jax.random.fold_in(key, 5)
    level_ids = jnp.arange(GLEVELS, dtype=jnp.float32) + 1.0
    scaling = (2.0 * NU / 2.0 ** level_ids) ** (-0.5)
    values = factor_values(key, (GLEVELS, 2, NS, K))
    return (values * scaling[:, None, None, None]).astype(jnp.bfloat16)


def draw_low_right(key, part):
    key = jax.random.fold_in(key, 9)
    level_ids = jnp.arange(MLEVELS, dtype=jnp.float32) + 1.0 + GLEVELS
    scaling = (2.0 * NU / 2.0 ** level_ids) ** (-0.5)
    values = factor_values(key, (MLEVELS, 2, NS, KM))
    return (values * scaling[:, None, None, None]).astype(jnp.bfloat16)


def shard_levels(own_key, dims, cuts, smallest, top_value):
    def one(dim, shards_of):
        draws = jax.random.uniform(jax.random.fold_in(jax.random.fold_in(own_key, 6), dim), (shards_of,), jnp.float32, smallest / len(cuts), top_value / len(cuts))
        return jnp.repeat(jnp.exp(draws), dims[dim] // shards_of).reshape((-1,) + (1,) * (len(dims) - dim - 1))

    factor_of = one(*cuts[0])
    for cut in cuts[1:]:
        factor_of = factor_of * one(*cut)
    return factor_of


def centred(own_key, dims, scale, most, pieces=(), kind=jnp.bfloat16):
    array = jax.random.normal(own_key, dims, jnp.float32) * scale
    if len(pieces) > 0:
        array = shard_levels(own_key, dims, pieces, -0.22, 0.18) * array
    return jnp.clip(array, min=-most, max=most).astype(kind)


def setup_inputs(seed: int = 0) -> dict:
    splits = jax.random.split(jax.random.key(seed), 10)
    return {
        "mesh_vector": centred(splits[0], (NU, COLS), 1.0, 6.0, ((0, 128),)),
        "cluster_position": draw_cluster_position(jax.random.fold_in(splits[9], 71), 0),
        "cluster_sizes": draw_cluster_sizes(jax.random.fold_in(splits[9], 71), 0),
        "block_ranks": draw_block_ranks(jax.random.fold_in(splits[9], 71), 0),
        "diag_block": centred(splits[4], (2, NS, CAP), (2 * CAP) ** -0.5, 0.09375, ((1, 128),)),
        "top_left": centred(splits[5], (GLEVELS, 2, NS, K), (2 * K) ** -0.5, 0.375, ((2, 128),)),
        "top_right": draw_top_right(jax.random.fold_in(splits[9], 71), 0),
        "low_left": centred(splits[7], (MLEVELS, 2, NS, KM), (2 * KM) ** -0.5, 0.5, ((2, 128),)),
        "low_right": draw_low_right(jax.random.fold_in(splits[9], 71), 0),
    }


def rotate(values):
    middle = values.shape[-1] // 2
    return jnp.concatenate([-values[..., middle:], values[..., :middle]], axis=-1)


def reference(mesh_vector, cluster_position, cluster_sizes, block_ranks, diag_block, top_left, top_right, low_left, low_right):
    leaves = cluster_sizes.shape[0]
    capacity = diag_block.shape[2]
    total_slots = leaves * capacity
    cluster_ends = jnp.cumsum(cluster_sizes).astype(jnp.int32)
    starts = (cluster_ends - cluster_sizes).astype(jnp.int32)
    owners = jnp.sum((cluster_position[:, None] >= cluster_ends[None, :]).astype(jnp.int32), axis=1)
    slot_ids = (owners * capacity + cluster_position - starts[owners]).astype(jnp.int32)
    values = jnp.zeros((total_slots, COLS), jnp.bfloat16).at[slot_ids].set(mesh_vector)
    turned = rotate(values)

    def diagonal_term(leaf_index):
        offset = (leaf_index * capacity).astype(jnp.int32)
        diag_piece = lax.dynamic_slice_in_dim(diag_block, offset, capacity, 1)
        plain = lax.dynamic_slice_in_dim(values, offset, capacity, 0)
        twisted = lax.dynamic_slice_in_dim(turned, offset, capacity, 0)
        return jnp.dot(diag_piece[0], plain, preferred_element_type=jnp.float32) + jnp.dot(diag_piece[1], twisted, preferred_element_type=jnp.float32)

    result = lax.map(diagonal_term, jnp.arange(leaves, dtype=jnp.int32)).reshape(total_slots, COLS)
    pair_full = jnp.stack([values, turned]).astype(jnp.float32)
    for tree_level in range(1, GLEVELS + MLEVELS + 1):
        if tree_level <= GLEVELS:
            right_factor = top_right[tree_level - 1]
            left_factor = top_left[tree_level - 1]
        else:
            right_factor = low_right[tree_level - 1 - GLEVELS]
            left_factor = low_left[tree_level - 1 - GLEVELS]
        nodes = 2 ** tree_level
        rank_cap = right_factor.shape[-1]
        node_rows = total_slots // nodes
        right_full = right_factor.astype(jnp.float32).reshape(2, nodes, node_rows, rank_cap)
        partial_value = jnp.einsum("pask,pasc->akc", right_full, pair_full.reshape(2, nodes, node_rows, COLS))
        sibling = partial_value.reshape(nodes // 2, 2, rank_cap, COLS)[:, ::-1].reshape(nodes, rank_cap, COLS)
        node_ranks = block_ranks[nodes - 2: 2 * nodes - 2]
        keep_mask = jnp.arange(rank_cap, dtype=jnp.int32)[None, :] < node_ranks[:, None]
        coefficient = jnp.where(keep_mask[:, :, None], sibling, 0.0).astype(jnp.bfloat16)
        coefficient_pair = jnp.stack([coefficient, rotate(coefficient)]).astype(jnp.float32)
        left_full = left_factor.astype(jnp.float32).reshape(2, nodes, node_rows, rank_cap)
        result = result + jnp.einsum("pask,pakc->asc", left_full, coefficient_pair).reshape(total_slots, COLS)
    return result[slot_ids]
```

```python
import jax
import jax.numpy as jnp
from jax import lax
from jax.experimental import pallas as pl
from jax.experimental.pallas import tpu as pltpu
from jax.sharding import PartitionSpec as P

LOGICAL = pl.DeviceIdType.LOGICAL
F32 = jnp.float32
BF16 = jnp.bfloat16
LEAVES = 128
LEVELS = 7
ROWS = 1024
CAP = 1792
BUCKET = 16
WINDOWS = CAP // 128
SLOTS = LEAVES * BUCKET
WIDTH = {1: 128, 2: 128, 3: 64, 4: 64, 5: 64, 6: 64, 7: 64}
START = {1: 0, 2: 128, 3: 256, 4: 320, 5: 384, 6: 448, 7: 512}
TOTAL = 576
OWNERS = {
    1: (16, 0, 4, 8),
    2: (16, 1, 2, 8),
    3: (4, 2, 4, 16),
    4: (8, 0, 1, 8),
    5: (4, 0, 1, 16),
    6: (2, 0, 1, 32),
    7: (1, 0, 1, 64),
}


def hops(step):
    ring = (0, 1, 2, 1)
    return ring[step >> 1 & 3] + ring[step >> 3 & 3] + ring[step >> 5 & 3]


def far_first(steps):
    return sorted(steps, key=lambda step: -hops(step))


def rotated(values):
    lane = lax.broadcasted_iota(jnp.int32, values.shape, 1)
    turned = pltpu.roll(values, 64, 1)
    return jnp.where(lane < 64, -turned, turned)


def one_hot(mask):
    return jnp.where(mask, 1.0, 0.0).astype(BF16)


def body(
    ranks,
    vector,
    position,
    sizes,
    diag_hbm,
    top_left_hbm,
    top_right_hbm,
    low_left_hbm,
    low_right_hbm,
    out,
    diag,
    top_right,
    low_left,
    right_t,
    left,
    spread,
    pick_t,
    put_t,
    sent,
    arrived,
    wide,
    field,
    partial,
    result,
    coef,
    returning,
    returned,
    *rest,
):
    sums = dict(zip(range(1, 8), rest[:7]))
    got = dict(zip(range(1, 7), rest[7:13]))
    load_sem, send_sem, row_sem, part_sem, coef_sem = rest[13:]
    me = lax.axis_index("group") * 32 + lax.axis_index("member")

    loads = {
        "right": [
            pltpu.make_async_copy(top_right_hbm, top_right, load_sem.at[0]),
        ]
        + [
            pltpu.make_async_copy(
                low_right_hbm.at[level, part],
                right_t.at[pl.ds(256 + level * 64, 64), pl.ds(part * CAP, CAP)],
                load_sem.at[11 + level * 2 + part],
            )
            for level in range(5)
            for part in range(2)
        ],
        "left": [pltpu.make_async_copy(low_left_hbm, low_left, load_sem.at[2])]
        + [
            pltpu.make_async_copy(
                top_left_hbm.at[level, part],
                left.at[:, pl.ds((level * 2 + part) * 128, 128)],
                load_sem.at[3 + level * 2 + part],
            )
            for level in range(2)
            for part in range(2)
        ],
        "diag": [
            pltpu.make_async_copy(
                diag_hbm.at[part, pl.ds(half * 896, 896)],
                diag.at[part, pl.ds(half * 896, 896)],
                load_sem.at[7 + part * 2 + half],
            )
            for part in range(2)
            for half in range(2)
        ],
    }
    for name in ("right", "left", "diag"):
        for copy in loads[name]:
            copy.start()

    barrier = pltpu.get_barrier_semaphore()
    everyone = far_first(range(1, LEAVES))
    for step in everyone:
        pl.semaphore_signal(barrier, inc=1, device_id=me ^ step, device_id_type=LOGICAL)

    sub = lax.broadcasted_iota(jnp.int32, (128, 128), 0)
    lane = lax.broadcasted_iota(jnp.int32, (128, 128), 1)
    size_rows = jnp.broadcast_to(sizes[...].astype(F32), (128, 128))
    ends = jnp.sum(jnp.where(lane <= sub, size_rows, 0.0), axis=1, keepdims=True)
    ends = jnp.broadcast_to(ends, (128, 128))
    where_rows, offset_rows = [], []
    for block in range(8):
        spot = position[pl.ds(block, 1), :]
        spots = jnp.broadcast_to(spot.astype(F32), (128, 128))
        past = spots >= ends
        owner = jnp.sum(jnp.where(past, 1.0, 0.0), axis=0, keepdims=True)
        begin = jnp.max(jnp.where(past, ends, 0.0), axis=0, keepdims=True)
        window = jnp.right_shift(spot, 7) - jnp.right_shift(begin.astype(jnp.int32), 7)
        where_rows.append(owner.astype(jnp.int32) * BUCKET + window)
        offset_rows.append(jnp.bitwise_and(spot, 127))
    where_cols = jnp.concatenate(where_rows, axis=0).astype(F32).T
    offset_cols = jnp.concatenate(offset_rows, axis=0).astype(F32).T
    for block in range(8):
        rows = pl.ds(block * 128, 128)
        spread[rows, pl.ds(0, 128)] = vector[rows, :]
        spread[rows, pl.ds(128, 128)] = jnp.broadcast_to(
            offset_cols[:, block : block + 1], (128, 128)
        ).astype(BF16)

    part_sub = lax.broadcasted_iota(jnp.int32, (256, 128), 0)
    bucket_row = lax.broadcasted_iota(jnp.int32, (16, 16, 128), 1)
    bucket_lane = lax.broadcasted_iota(jnp.int32, (16, 16, 128), 2)
    for chunk in range(SLOTS // 256):
        picks = jnp.concatenate(
            [one_hot(part_sub + chunk * 256 == where_rows[block]) for block in range(8)], axis=1
        )
        both = jnp.dot(picks, spread[...], preferred_element_type=F32)
        data = both[:, :128].reshape(16, 16, 128)
        offsets = both[:, 128:].reshape(16, 16, 128)
        row = jnp.sum(
            jnp.where(bucket_row == bucket_lane, offsets, 0.0), axis=1, keepdims=True
        )
        data = jnp.where(bucket_row == 14, row, data)
        sent[pl.ds(chunk * 256, 256), :] = data.reshape(256, 128).astype(BF16)

    pl.semaphore_wait(barrier, LEAVES - 1)

    def bucket(index):
        return pl.ds(pl.multiple_of(index * BUCKET, BUCKET), BUCKET)

    for step in everyone:
        other = me ^ step
        pltpu.make_async_remote_copy(
            sent.at[bucket(other)],
            arrived.at[bucket(me)],
            send_sem.at[0],
            row_sem.at[0],
            device_id=other,
            device_id_type=LOGICAL,
        ).start()
    arrived[bucket(me), :] = sent[bucket(me), :]

    for copy in loads["right"]:
        copy.wait()

    @pl.loop(0, WINDOWS)
    def _(window):
        rows = pl.ds(pl.multiple_of(window * 128, 128), 128)
        for part in range(2):
            columns = pl.ds(pl.multiple_of(part * CAP + window * 128, 128), 128)
            for level in range(2):
                right_t[pl.ds(level * 128, 128), columns] = top_right[level, part, rows, :].T

    for copy in loads["left"]:
        copy.wait()

    @pl.loop(0, WINDOWS)
    def _(window):
        rows = pl.ds(pl.multiple_of(window * 128, 128), 128)
        for level in range(5):
            left[rows, pl.ds(512 + level * 128, 128)] = low_left[level, :, rows].T

    for block in range(8):
        column = jnp.broadcast_to(where_cols[:, block : block + 1], (128, 128)).astype(jnp.int32)
        for piece in range(SLOTS // 128):
            pick_t[pl.ds(block * 128, 128), pl.ds(piece * 128, 128)] = one_hot(
                column == lane + piece * 128
            )

    def landed(buffer, rows, semaphore):
        view = buffer.at[pl.ds(0, rows)]
        pltpu.make_async_copy(view, view, semaphore).wait()

    landed(arrived, SLOTS - BUCKET, row_sem.at[0])

    wide[...] = arrived[...].astype(F32)
    offsets = wide[pl.ds(14, 128, stride=16), :]
    offsets_t = offsets.T
    sub_f = sub.astype(F32)
    lane_f = lane.astype(F32)
    for window in range(WINDOWS):
        put = one_hot(jnp.broadcast_to(offsets_t[window : window + 1, :], (128, 128)) == sub_f)
        rows = wide[pl.ds(window, 128, stride=16), :].astype(BF16)
        values = jnp.dot(put, rows, preferred_element_type=F32)
        field[pl.ds(window * 128, 128), :] = values.astype(BF16)
        field[pl.ds(CAP + window * 128, 128), :] = rotated(values).astype(BF16)

    for level in range(1, 8):
        count, first, apart, rows = OWNERS[level]
        members = 1 << (LEVELS - level)
        begin, width = START[level], WIDTH[level]
        partial[pl.ds(begin, width), :] = jnp.dot(
            right_t[pl.ds(begin, width), :], field[...], preferred_element_type=F32
        )
        node = ((me >> (LEVELS - level)) ^ 1) << (LEVELS - level)
        place = me & (members - 1)
        for step in far_first(range(count)):
            index = (place // apart) ^ step
            pltpu.make_async_remote_copy(
                partial.at[pl.ds(pl.multiple_of(begin + index * rows, 8), rows)],
                sums[level].at[pl.ds(pl.multiple_of(place * rows, 8), rows)],
                send_sem.at[1],
                part_sem.at[level - 1],
                device_id=node + first + index * apart,
                device_id_type=LOGICAL,
            ).start()

    for copy in loads["diag"]:
        copy.wait()

    @pl.loop(0, CAP // 256)
    def _(chunk):
        rows = pl.ds(pl.multiple_of(chunk * 256, 256), 256)
        result[rows, :] = jnp.dot(
            diag[0, rows, :], field[pl.ds(0, CAP), :], preferred_element_type=F32
        ) + jnp.dot(diag[1, rows, :], field[pl.ds(CAP, CAP), :], preferred_element_type=F32)

    for window in range(WINDOWS):
        column = jnp.broadcast_to(offsets[:, window : window + 1], (128, 128))
        put_t[pl.ds(window * 128, 128), :] = one_hot(column == lane_f)

    for level in range(1, 7):
        count, first, apart, rows = OWNERS[level]
        members = 1 << (LEVELS - level)
        place = me & (members - 1)
        index = place // apart

        @pl.when(place % apart == first)
        def _(level=level, rows=rows, members=members, index=index):
            landed(sums[level], members * rows, part_sem.at[level - 1])
            total = jnp.sum(sums[level][...].reshape(members, rows, 128), axis=0)
            rank = ranks[(1 << level) - 2 + (me >> (LEVELS - level))]
            row = lax.broadcasted_iota(jnp.int32, (rows, 128), 0) + index * rows
            mine = pl.ds(pl.multiple_of(index * rows, 8), rows)
            got[level][mine, :] = jnp.where(row < rank, total, 0.0)
            for step in far_first(range(1, members)):
                pltpu.make_async_remote_copy(
                    got[level].at[mine],
                    got[level].at[mine],
                    send_sem.at[2],
                    coef_sem.at[level - 1],
                    device_id=me ^ step,
                    device_id_type=LOGICAL,
                ).start()

    def set_coef(level, values):
        begin = START[level] * 2
        width = WIDTH[level]
        values = values.astype(BF16).astype(F32)
        coef[pl.ds(begin, width), :] = values.astype(BF16)
        coef[pl.ds(begin + width, width), :] = rotated(values).astype(BF16)

    landed(sums[7], 64, part_sem.at[6])
    row = lax.broadcasted_iota(jnp.int32, (64, 128), 0)
    set_coef(7, jnp.where(row < ranks[(1 << 7) - 2 + me], sums[7][...], 0.0))
    for level in range(6, 0, -1):
        count, first, apart, rows = OWNERS[level]
        members = 1 << (LEVELS - level)
        owner = (me & (members - 1)) % apart == first

        @pl.when(owner)
        def _(level=level, rows=rows):
            landed(got[level], WIDTH[level] - rows, coef_sem.at[level - 1])

        if apart > 1:

            @pl.when(jnp.logical_not(owner))
            def _(level=level):
                landed(got[level], WIDTH[level], coef_sem.at[level - 1])

        set_coef(level, got[level][...])

    wide[pl.ds(14, 128, stride=16), :] = jnp.zeros((128, 128), F32)
    wide[pl.ds(15, 128, stride=16), :] = jnp.zeros((128, 128), F32)
    for chunk in range(CAP // 256):
        rows = pl.ds(chunk * 256, 256)
        values = result[rows, :] + jnp.dot(left[rows, :], coef[...], preferred_element_type=F32)
        values = values.astype(BF16)
        for half in range(2):
            window = chunk * 2 + half
            wide[pl.ds(window, 128, stride=16), :] = jnp.dot(
                put_t[pl.ds(window * 128, 128), :],
                values[half * 128 : half * 128 + 128],
                preferred_element_type=F32,
            )
    returning[...] = wide[...].astype(BF16)
    for step in everyone:
        other = me ^ step
        pltpu.make_async_remote_copy(
            returning.at[bucket(other)],
            returned.at[bucket(me)],
            send_sem.at[3],
            row_sem.at[1],
            device_id=other,
            device_id_type=LOGICAL,
        ).start()
    returned[bucket(me), :] = returning[bucket(me), :]

    landed(sent, SLOTS - BUCKET, send_sem.at[0])
    landed(partial, TOTAL, send_sem.at[1])
    for level in range(1, 7):
        count, first, apart, rows = OWNERS[level]
        members = 1 << (LEVELS - level)

        @pl.when((me & (members - 1)) % apart == first)
        def _(level=level, rows=rows, members=members):
            landed(sums[level], (members - 1) * rows, send_sem.at[2])

    landed(returned, SLOTS - BUCKET, row_sem.at[1])

    @pl.loop(0, ROWS // 256)
    def _(chunk):
        rows = pl.ds(pl.multiple_of(chunk * 256, 256), 256)
        out[rows, :] = jnp.dot(pick_t[rows, :], returned[...], preferred_element_type=F32)

    landed(returning, SLOTS - BUCKET, send_sem.at[3])


def on_device(
    mesh_vector,
    cluster_position,
    cluster_sizes,
    block_ranks,
    diag_block,
    top_left,
    top_right,
    low_left,
    low_right,
):
    vmem = pl.BlockSpec(memory_space=pltpu.VMEM)
    anywhere = pl.BlockSpec(memory_space=pl.ANY)
    scratch = [
        pltpu.VMEM((2, CAP, CAP), BF16),
        pltpu.VMEM((2, 2, CAP, 128), BF16),
        pltpu.VMEM((5, 128, CAP), BF16),
        pltpu.VMEM((TOTAL, 2 * CAP), BF16),
        pltpu.VMEM((CAP, 2 * TOTAL), BF16),
        pltpu.VMEM((ROWS, 256), BF16),
        pltpu.VMEM((ROWS, SLOTS), BF16),
        pltpu.VMEM((CAP, 128), BF16),
        pltpu.VMEM((SLOTS, 128), BF16),
        pltpu.VMEM((SLOTS, 128), BF16),
        pltpu.VMEM((SLOTS, 128), F32),
        pltpu.VMEM((2 * CAP, 128), BF16),
        pltpu.VMEM((TOTAL, 128), F32),
        pltpu.VMEM((CAP, 128), F32),
        pltpu.VMEM((2 * TOTAL, 128), BF16),
        pltpu.VMEM((SLOTS, 128), BF16),
        pltpu.VMEM((SLOTS, 128), BF16),
    ]
    scratch += [
        pltpu.VMEM(((1 << (LEVELS - level)) * OWNERS[level][3], 128), F32) for level in range(1, 8)
    ]
    scratch += [pltpu.VMEM((WIDTH[level], 128), F32) for level in range(1, 7)]
    scratch += [
        pltpu.SemaphoreType.DMA((21,)),
        pltpu.SemaphoreType.DMA((4,)),
        pltpu.SemaphoreType.DMA((2,)),
        pltpu.SemaphoreType.DMA((7,)),
        pltpu.SemaphoreType.DMA((6,)),
    ]
    return pl.pallas_call(
        body,
        out_shape=jax.ShapeDtypeStruct((ROWS, 128), F32),
        in_specs=[pl.BlockSpec(memory_space=pltpu.SMEM), vmem, vmem, vmem] + [anywhere] * 5,
        out_specs=vmem,
        scratch_shapes=scratch,
        compiler_params=pltpu.CompilerParams(
            collective_id=0, has_side_effects=True, vmem_limit_bytes=56 * 2**20
        ),
        name="tree_product",
    )(
        block_ranks,
        mesh_vector,
        cluster_position.reshape(8, 128),
        cluster_sizes.reshape(1, 128),
        diag_block,
        top_left,
        top_right,
        jnp.swapaxes(low_left, 2, 3).reshape(5, 128, CAP),
        jnp.swapaxes(low_right, 2, 3),
    )


def solution(mesh):
    return jax.shard_map(
        on_device,
        mesh=mesh,
        in_specs=(
            P(("group", "member"), None),
            P(("group", "member")),
            P(),
            P(),
            P(None, ("group", "member"), None),
            P(None, None, ("group", "member"), None),
            P(None, None, ("group", "member"), None),
            P(None, None, ("group", "member"), None),
            P(None, None, ("group", "member"), None),
        ),
        out_specs=P(("group", "member"), None),
        check_vma=False,
    )
```

```python
import jax
import jax.numpy as jnp
from jax import lax
from jax.experimental import pallas as pl
from jax.experimental.pallas import tpu as pltpu
from jax.sharding import PartitionSpec as P

LOGICAL = pl.DeviceIdType.LOGICAL
F32 = jnp.float32
BF16 = jnp.bfloat16
LEAVES = 128
LEVELS = 7
ROWS = 1024
CAP = 1792
BUCKET = 16
WINDOWS = CAP // 128
SLOTS = LEAVES * BUCKET
WIDTH = {1: 128, 2: 128, 3: 64, 4: 64, 5: 64, 6: 64, 7: 64}
START = {1: 0, 2: 128, 3: 256, 4: 320, 5: 384, 6: 448, 7: 512}
TOTAL = 576
TURNS = (0, 32, 64, 96, 128)
OWNERS = {
    1: (8, 0, 4, 16),
    2: (8, 1, 4, 16),
    3: (4, 2, 4, 16),
    4: (4, 1, 2, 16),
    5: (4, 0, 1, 16),
    6: (2, 0, 1, 32),
    7: (1, 0, 1, 64),
}


def hops(step):
    ring = (0, 1, 2, 1)
    return ring[step >> 1 & 3] + ring[step >> 3 & 3] + ring[step >> 5 & 3]


def far_first(steps):
    return sorted(steps, key=lambda step: -hops(step))


def sources_of(level):
    return 1 << (LEVELS - level)


def region_of(level):
    return min(sources_of(level), 32)


def turn_of(place):
    return sum(place >= begin for begin in TURNS[1:-1])


def rotated(values):
    lane = lax.broadcasted_iota(jnp.int32, values.shape, 1)
    turned = pltpu.roll(values, 64, 1)
    return jnp.where(lane < 64, -turned, turned)


def one_hot(mask):
    return jnp.where(mask, 1.0, 0.0).astype(BF16)


def body(
    ranks_hbm,
    vector_hbm,
    position_hbm,
    sizes_hbm,
    diag_hbm,
    top_left_hbm,
    top_right_hbm,
    low_left_hbm,
    low_right_hbm,
    product,
    ranks,
    vector,
    position,
    sizes,
    diag,
    top_right,
    low_left,
    right_t,
    left,
    spread,
    pick_t,
    put_t,
    sent,
    arrived,
    wide,
    field,
    partial,
    result,
    coef,
    returning,
    returned,
    *rest,
):
    sums = dict(zip(range(1, 8), rest[:7]))
    got = dict(zip(range(1, 7), rest[7:13]))
    load_sem, send_sem, row_sem, part_sem, coef_sem = rest[13:]
    me = lax.axis_index("group") * 32 + lax.axis_index("member")

    first_loads = [
        pltpu.make_async_copy(source, target, load_sem.at[21 + index])
        for index, (source, target) in enumerate(
            (
                (position_hbm, position),
                (sizes_hbm, sizes),
                (vector_hbm, vector),
                (ranks_hbm, ranks),
            )
        )
    ]
    for copy in first_loads:
        copy.start()
    barrier = pltpu.get_barrier_semaphore()
    everyone = far_first(range(1, LEAVES))
    for step in everyone:
        pl.semaphore_signal(barrier, inc=1, device_id=me ^ step, device_id_type=LOGICAL)

    loads = {
        "right": [
            pltpu.make_async_copy(top_right_hbm, top_right, load_sem.at[0]),
        ]
        + [
            pltpu.make_async_copy(
                low_right_hbm.at[level, part],
                right_t.at[pl.ds(256 + level * 64, 64), pl.ds(part * CAP, CAP)],
                load_sem.at[11 + level * 2 + part],
            )
            for level in range(5)
            for part in range(2)
        ],
        "left": [pltpu.make_async_copy(low_left_hbm, low_left, load_sem.at[2])]
        + [
            pltpu.make_async_copy(
                top_left_hbm.at[level, part],
                left.at[:, pl.ds((level * 2 + part) * 128, 128)],
                load_sem.at[3 + level * 2 + part],
            )
            for level in range(2)
            for part in range(2)
        ],
        "diag": [
            pltpu.make_async_copy(
                diag_hbm.at[part, pl.ds(half * 896, 896)],
                diag.at[part, pl.ds(half * 896, 896)],
                load_sem.at[7 + part * 2 + half],
            )
            for part in range(2)
            for half in range(2)
        ],
    }
    for name in ("right", "left", "diag"):
        for copy in loads[name]:
            copy.start()
    for copy in first_loads:
        copy.wait()

    sub = lax.broadcasted_iota(jnp.int32, (128, 128), 0)
    lane = lax.broadcasted_iota(jnp.int32, (128, 128), 1)
    size_rows = jnp.broadcast_to(sizes[...].astype(F32), (128, 128))
    ends = jnp.sum(jnp.where(lane <= sub, size_rows, 0.0), axis=1, keepdims=True)
    ends = jnp.broadcast_to(ends, (128, 128))
    where_rows, window_rows, owner_rows, offset_rows = [], [], [], []
    for block in range(8):
        spot = position[pl.ds(block, 1), :]
        spots = jnp.broadcast_to(spot.astype(F32), (128, 128))
        past = spots >= ends
        owner = jnp.sum(jnp.where(past, 1.0, 0.0), axis=0, keepdims=True)
        begin = jnp.max(jnp.where(past, ends, 0.0), axis=0, keepdims=True)
        window = jnp.right_shift(spot, 7) - jnp.right_shift(begin.astype(jnp.int32), 7)
        owner_rows.append(owner)
        window_rows.append(window)
        where_rows.append(owner.astype(jnp.int32) * BUCKET + window)
        offset_rows.append(jnp.bitwise_and(spot, 127))
    offset_cols = jnp.concatenate(offset_rows, axis=0).astype(F32).T
    for block in range(8):
        rows = pl.ds(block * 128, 128)
        spread[rows, pl.ds(0, 128)] = vector[rows, :]
        spread[rows, pl.ds(128, 128)] = jnp.broadcast_to(
            offset_cols[:, block : block + 1], (128, 128)
        ).astype(BF16)

    part_sub = lax.broadcasted_iota(jnp.int32, (256, 128), 0)
    bucket_row = lax.broadcasted_iota(jnp.int32, (16, 16, 128), 1)
    bucket_lane = lax.broadcasted_iota(jnp.int32, (16, 16, 128), 2)
    for chunk in range(SLOTS // 256):
        picks = jnp.concatenate(
            [one_hot(part_sub + chunk * 256 == where_rows[block]) for block in range(8)], axis=1
        )
        both = jnp.dot(picks, spread[...], preferred_element_type=F32)
        data = both[:, :128].reshape(16, 16, 128)
        offsets = both[:, 128:].reshape(16, 16, 128)
        row = jnp.sum(
            jnp.where(bucket_row == bucket_lane, offsets, 0.0), axis=1, keepdims=True
        )
        data = jnp.where(bucket_row == 14, row, data)
        sent[pl.ds(chunk * 256, 256), :] = data.reshape(256, 128).astype(BF16)

    pl.semaphore_wait(barrier, LEAVES - 1)

    def bucket(index):
        return pl.ds(pl.multiple_of(index * BUCKET, BUCKET), BUCKET)

    for step in everyone:
        other = me ^ step
        pltpu.make_async_remote_copy(
            sent.at[bucket(other)],
            arrived.at[bucket(me)],
            send_sem.at[0],
            row_sem.at[0],
            device_id=other,
            device_id_type=LOGICAL,
        ).start()
    arrived[bucket(me), :] = sent[bucket(me), :]

    for copy in loads["right"]:
        copy.wait()

    @pl.loop(0, WINDOWS)
    def _(window):
        rows = pl.ds(pl.multiple_of(window * 128, 128), 128)
        for part in range(2):
            columns = pl.ds(pl.multiple_of(part * CAP + window * 128, 128), 128)
            for level in range(2):
                right_t[pl.ds(level * 128, 128), columns] = top_right[level, part, rows, :].T

    for copy in loads["left"]:
        copy.wait()

    @pl.loop(0, WINDOWS)
    def _(window):
        rows = pl.ds(pl.multiple_of(window * 128, 128), 128)
        for level in range(5):
            left[rows, pl.ds(512 + level * 128, 128)] = low_left[level, :, rows].T

    steps = jnp.bitwise_xor(lax.broadcasted_iota(jnp.int32, (1, 128), 1), me)
    places = jnp.full((1, 128), LEAVES - 1, jnp.int32)
    for place, step in enumerate(everyone):
        places = jnp.where(steps == step, place, places)
    places = jnp.broadcast_to(places.astype(F32), (128, 128)).T
    where_back = []
    for block in range(8):
        owners = jnp.broadcast_to(owner_rows[block], (128, 128)).astype(jnp.int32)
        place = jnp.sum(jnp.where(owners == sub, places, 0.0), axis=0, keepdims=True)
        where_back.append(place * BUCKET + window_rows[block].astype(F32))
    where_back = jnp.concatenate(where_back, axis=0).T
    for block in range(8):
        column = jnp.broadcast_to(where_back[:, block : block + 1], (128, 128)).astype(jnp.int32)
        for piece in range(SLOTS // 128):
            pick_t[pl.ds(block * 128, 128), pl.ds(piece * 128, 128)] = one_hot(
                column == lane + piece * 128
            )

    def landed(buffer, rows, semaphore):
        view = buffer.at[pl.ds(0, rows)]
        pltpu.make_async_copy(view, view, semaphore).wait()

    landed(arrived, SLOTS - BUCKET, row_sem.at[0])

    wide[...] = arrived[...].astype(F32)
    offsets = wide[pl.ds(14, 128, stride=16), :]
    offsets_t = offsets.T
    sub_f = sub.astype(F32)
    lane_f = lane.astype(F32)
    for window in range(WINDOWS):
        put = one_hot(jnp.broadcast_to(offsets_t[window : window + 1, :], (128, 128)) == sub_f)
        rows = wide[pl.ds(window, 128, stride=16), :].astype(BF16)
        values = jnp.dot(put, rows, preferred_element_type=F32)
        field[pl.ds(window * 128, 128), :] = values.astype(BF16)
        field[pl.ds(CAP + window * 128, 128), :] = rotated(values).astype(BF16)

    for levels in ((1, 2), (3, 4, 5, 6, 7)):
        span = pl.ds(START[levels[0]], sum(WIDTH[level] for level in levels))
        partial[span, :] = jnp.dot(right_t[span, :], field[...], preferred_element_type=F32)
        for level in levels:
            count, first, apart, rows = OWNERS[level]
            node = ((me >> (LEVELS - level)) ^ 1) << (LEVELS - level)
            place = me & (sources_of(level) - 1)
            index = (place & (region_of(level) - 1)) // apart
            for group in range(sources_of(level) // region_of(level)):
                for step in far_first(range(count)):
                    piece = index ^ step
                    pltpu.make_async_remote_copy(
                        partial.at[pl.ds(pl.multiple_of(START[level] + piece * rows, 8), rows)],
                        sums[level].at[pl.ds(pl.multiple_of(place * rows, 8), rows)],
                        send_sem.at[1],
                        part_sem.at[level - 1],
                        device_id=node + group * 32 + first + piece * apart,
                        device_id_type=LOGICAL,
                    ).start()

    for copy in loads["diag"]:
        copy.wait()

    @pl.loop(0, CAP // 256)
    def _(chunk):
        rows = pl.ds(pl.multiple_of(chunk * 256, 256), 256)
        result[rows, :] = jnp.dot(
            diag[0, rows, :], field[pl.ds(0, CAP), :], preferred_element_type=F32
        ) + jnp.dot(diag[1, rows, :], field[pl.ds(CAP, CAP), :], preferred_element_type=F32)

    for window in range(WINDOWS):
        column = jnp.broadcast_to(offsets[:, window : window + 1], (128, 128))
        rows = pl.ds(window * 128, 128)
        put_t[rows, pl.ds(window % 2 * 128, 128)] = one_hot(column == lane_f)
        put_t[rows, pl.ds(128 - window % 2 * 128, 128)] = jnp.zeros((128, 128), BF16)
    wide[pl.ds(14, 128, stride=16), :] = jnp.zeros((128, 128), F32)
    wide[pl.ds(15, 128, stride=16), :] = jnp.zeros((128, 128), F32)

    for level in range(6, 0, -1):
        count, first, apart, rows = OWNERS[level]
        place = me & (region_of(level) - 1)

        @pl.when(place % apart == first)
        def _(level=level, rows=rows, index=place // apart):
            sources = sources_of(level)
            landed(sums[level], sources * rows, part_sem.at[level - 1])
            total = jnp.sum(sums[level][...].reshape(sources, rows, 128), axis=0)
            rank = ranks[(1 << level) - 2 + (me >> (LEVELS - level))]
            row = lax.broadcasted_iota(jnp.int32, (rows, 128), 0) + index * rows
            mine = pl.ds(pl.multiple_of(index * rows, 16), rows)
            got[level][mine, :] = jnp.where(row < rank, total, 0.0).astype(BF16)
            for step in far_first(range(1, region_of(level))):
                pltpu.make_async_remote_copy(
                    got[level].at[mine],
                    got[level].at[mine],
                    send_sem.at[2],
                    coef_sem.at[level - 1],
                    device_id=me ^ step,
                    device_id_type=LOGICAL,
                ).start()

    def set_coef(level, values):
        begin = START[level] * 2
        width = WIDTH[level]
        coef[pl.ds(begin, width), :] = values
        coef[pl.ds(begin + width, width), :] = rotated(values.astype(F32)).astype(BF16)

    landed(sums[7], 64, part_sem.at[6])
    row = lax.broadcasted_iota(jnp.int32, (64, 128), 0)
    set_coef(7, jnp.where(row < ranks[(1 << 7) - 2 + me], sums[7][...], 0.0).astype(BF16))

    def await_coef(level):
        count, first, apart, rows = OWNERS[level]
        owner = (me & (region_of(level) - 1)) % apart == first

        @pl.when(owner)
        def _():
            landed(got[level], WIDTH[level] - rows, coef_sem.at[level - 1])

        if apart > 1:

            @pl.when(jnp.logical_not(owner))
            def _():
                landed(got[level], WIDTH[level], coef_sem.at[level - 1])

        set_coef(level, got[level][...])

    for level in range(6, 2, -1):
        await_coef(level)
    for chunk in range(CAP // 256):
        rows = pl.ds(chunk * 256, 256)
        result[rows, :] += jnp.dot(
            left[rows, pl.ds(512, 640)], coef[pl.ds(512, 640), :], preferred_element_type=F32
        )
    for level in (2, 1):
        await_coef(level)

    for chunk in range(CAP // 256):
        rows = pl.ds(chunk * 256, 256)
        values = result[rows, :] + jnp.dot(
            left[rows, pl.ds(0, 512)], coef[pl.ds(0, 512), :], preferred_element_type=F32
        )
        field[rows, :] = values.astype(BF16)
    for chunk in range(CAP // 256):
        rows = pl.ds(chunk * 256, 256)
        leaving = jnp.dot(put_t[rows, :], field[rows, :], preferred_element_type=F32)
        for half in range(2):
            wide[pl.ds(chunk * 2 + half, 128, stride=16), :] = leaving[half * 128 : half * 128 + 128]
    returning[...] = wide[...].astype(BF16)
    for place, step in enumerate(everyone):
        other = me ^ step
        pltpu.make_async_remote_copy(
            returning.at[bucket(other)],
            returned.at[pl.ds(place * BUCKET, BUCKET)],
            send_sem.at[3],
            row_sem.at[1 + turn_of(place)],
            device_id=other,
            device_id_type=LOGICAL,
        ).start()
    returned[pl.ds(SLOTS - BUCKET, BUCKET), :] = returning[bucket(me), :]

    landed(sent, SLOTS - BUCKET, send_sem.at[0])
    landed(partial, TOTAL, send_sem.at[1])
    landed(partial, WIDTH[1], send_sem.at[1])
    for level in range(1, 7):
        count, first, apart, rows = OWNERS[level]

        @pl.when((me & (region_of(level) - 1)) % apart == first)
        def _(level=level, rows=rows):
            landed(sent, (region_of(level) - 1) * rows, send_sem.at[2])

    for turn, (begin, end) in enumerate(zip(TURNS[:-1], TURNS[1:])):
        count = (end - begin) * BUCKET
        landed(returned, count - BUCKET if end == LEAVES else count, row_sem.at[1 + turn])
        span = pl.ds(begin * BUCKET, count)
        for chunk in range(ROWS // 256):
            rows = pl.ds(chunk * 256, 256)
            total = jnp.dot(pick_t[rows, span], returned[span, :], preferred_element_type=F32)
            if turn > 0:
                total += result[rows, :]
            if end < LEAVES:
                result[rows, :] = total
            else:
                product[rows, :] = total.astype(BF16)
    landed(returning, SLOTS - BUCKET, send_sem.at[3])


def on_device(
    mesh_vector,
    cluster_position,
    cluster_sizes,
    block_ranks,
    diag_block,
    top_left,
    top_right,
    low_left,
    low_right,
):
    scratch = [
        pltpu.SMEM((254,), jnp.int32),
        pltpu.VMEM((ROWS, 128), BF16),
        pltpu.VMEM((8, 128), jnp.int32),
        pltpu.VMEM((1, 128), jnp.int32),
        pltpu.VMEM((2, CAP, CAP), BF16),
        pltpu.VMEM((2, 2, CAP, 128), BF16),
        pltpu.VMEM((5, 128, CAP), BF16),
        pltpu.VMEM((TOTAL, 2 * CAP), BF16),
        pltpu.VMEM((CAP, 2 * TOTAL), BF16),
        pltpu.VMEM((ROWS, 256), BF16),
        pltpu.VMEM((ROWS, SLOTS), BF16),
        pltpu.VMEM((CAP, 256), BF16),
        pltpu.VMEM((SLOTS, 128), BF16),
        pltpu.VMEM((SLOTS, 128), BF16),
        pltpu.VMEM((SLOTS, 128), F32),
        pltpu.VMEM((2 * CAP, 128), BF16),
        pltpu.VMEM((TOTAL, 128), F32),
        pltpu.VMEM((CAP, 128), F32),
        pltpu.VMEM((2 * TOTAL, 128), BF16),
        pltpu.VMEM((SLOTS, 128), BF16),
        pltpu.VMEM((SLOTS, 128), BF16),
    ]
    scratch += [
        pltpu.VMEM(((1 << (LEVELS - level)) * OWNERS[level][3], 128), F32) for level in range(1, 8)
    ]
    scratch += [pltpu.VMEM((WIDTH[level], 128), BF16) for level in range(1, 7)]
    scratch += [
        pltpu.SemaphoreType.DMA((25,)),
        pltpu.SemaphoreType.DMA((4,)),
        pltpu.SemaphoreType.DMA((5,)),
        pltpu.SemaphoreType.DMA((7,)),
        pltpu.SemaphoreType.DMA((6,)),
    ]
    product = pl.pallas_call(
        body,
        out_shape=pltpu.VMEM((ROWS, 128), BF16),
        in_specs=[pl.BlockSpec(memory_space=pltpu.HBM)] * 9,
        out_specs=pl.BlockSpec(memory_space=pltpu.VMEM),
        scratch_shapes=scratch,
        compiler_params=pltpu.CompilerParams(
            collective_id=0, has_side_effects=True, vmem_limit_bytes=53 * 2**20
        ),
        name="tree_product",
    )(*(pltpu.with_memory_space_constraint(operand, pltpu.HBM) for operand in (
        block_ranks,
        mesh_vector,
        cluster_position.reshape(8, 128),
        cluster_sizes.reshape(1, 128),
        diag_block,
        top_left,
        top_right,
        jnp.swapaxes(low_left, 2, 3).reshape(5, 128, CAP),
        jnp.swapaxes(low_right, 2, 3),
    )))
    return product.astype(F32)


def solution(mesh):
    return jax.shard_map(
        on_device,
        mesh=mesh,
        in_specs=(
            P(("group", "member"), None),
            P(("group", "member")),
            P(),
            P(),
            P(None, ("group", "member"), None),
            P(None, None, ("group", "member"), None),
            P(None, None, ("group", "member"), None),
            P(None, None, ("group", "member"), None),
            P(None, None, ("group", "member"), None),
        ),
        out_specs=P(("group", "member"), None),
        check_vma=False,
    )
```

```python
import jax
import jax.numpy as jnp
from jax import lax
from jax.experimental import pallas as pl
from jax.experimental.pallas import tpu as pltpu
from jax.sharding import PartitionSpec as P

LOGICAL = pl.DeviceIdType.LOGICAL
F32 = jnp.float32
BF16 = jnp.bfloat16
LEAVES = 128
LEVELS = 7
ROWS = 1024
CAP = 1792
BUCKET = 16
WINDOWS = CAP // 128
SLOTS = LEAVES * BUCKET
WIDTH = {1: 128, 2: 128, 3: 64, 4: 64, 5: 64, 6: 64, 7: 64}
START = {1: 0, 2: 128, 3: 256, 4: 320, 5: 384, 6: 448, 7: 512}
TOTAL = 576
TURNS = (0, 32, 64, 96, 128)
OWNERS = {
    1: (16, 0, 4, 8),
    2: (8, 3, 4, 16),
    3: (4, 1, 4, 16),
    4: (4, 1, 2, 16),
    5: (4, 0, 1, 16),
    6: (2, 0, 1, 32),
    7: (1, 0, 1, 64),
}


def hops(step):
    ring = (0, 1, 2, 1)
    return ring[step >> 1 & 3] + ring[step >> 3 & 3] + ring[step >> 5 & 3]


def far_first(steps):
    return sorted(steps, key=lambda step: (-hops(step), -(step & 1)))


def sources_of(level):
    return 1 << (LEVELS - level)


def sum_type(level):
    return BF16 if OWNERS[level][3] >= 16 else F32


def turn_of(place):
    return sum(place >= begin for begin in TURNS[1:-1])


def rotated(values):
    lane = lax.broadcasted_iota(jnp.int32, values.shape, 1)
    turned = pltpu.roll(values, 64, 1)
    return jnp.where(lane < 64, -turned, turned)


def one_hot(mask):
    return jnp.where(mask, 1.0, 0.0).astype(BF16)


def body(
    ranks_hbm,
    vector_hbm,
    position_hbm,
    sizes_hbm,
    diag_hbm,
    top_left_hbm,
    top_right_hbm,
    low_left_hbm,
    low_right_hbm,
    product,
    ranks,
    vector,
    position,
    sizes,
    diag,
    top_right,
    low_left,
    right_t,
    left,
    spread,
    pick_t,
    put_t,
    sent,
    arrived,
    wide,
    field,
    partial,
    result,
    coef,
    returning,
    returned,
    *rest,
):
    sums = dict(zip(range(1, 8), rest[:7]))
    got = dict(zip(range(1, 7), rest[7:13]))
    load_sem, send_sem, row_sem, part_sem, coef_sem = rest[13:]
    me = lax.axis_index("group") * 32 + lax.axis_index("member")

    first_loads = [
        pltpu.make_async_copy(source, target, load_sem.at[21 + index])
        for index, (source, target) in enumerate(
            (
                (position_hbm, position),
                (sizes_hbm, sizes),
                (vector_hbm, vector),
                (ranks_hbm, ranks),
            )
        )
    ]
    for copy in first_loads:
        copy.start()
    barrier = pltpu.get_barrier_semaphore()
    everyone = far_first(range(1, LEAVES))
    for step in everyone:
        pl.semaphore_signal(barrier, inc=1, device_id=me ^ step, device_id_type=LOGICAL)

    loads = {
        "right": [
            pltpu.make_async_copy(top_right_hbm, top_right, load_sem.at[0]),
        ]
        + [
            pltpu.make_async_copy(
                low_right_hbm.at[level, part],
                right_t.at[pl.ds(256 + level * 64, 64), pl.ds(part * CAP, CAP)],
                load_sem.at[11 + level * 2 + part],
            )
            for level in range(5)
            for part in range(2)
        ],
        "left": [pltpu.make_async_copy(low_left_hbm, low_left, load_sem.at[2])]
        + [
            pltpu.make_async_copy(
                top_left_hbm.at[level, part],
                left.at[:, pl.ds((level * 2 + part) * 128, 128)],
                load_sem.at[3 + level * 2 + part],
            )
            for level in range(2)
            for part in range(2)
        ],
        "diag": [
            pltpu.make_async_copy(
                diag_hbm.at[part, pl.ds(half * 896, 896)],
                diag.at[part, pl.ds(half * 896, 896)],
                load_sem.at[7 + part * 2 + half],
            )
            for part in range(2)
            for half in range(2)
        ],
    }
    for name in ("right", "left", "diag"):
        for copy in loads[name]:
            copy.start()
    for copy in first_loads:
        copy.wait()

    sub = lax.broadcasted_iota(jnp.int32, (128, 128), 0)
    lane = lax.broadcasted_iota(jnp.int32, (128, 128), 1)
    size_rows = jnp.broadcast_to(sizes[...].astype(F32), (128, 128))
    ends = jnp.sum(jnp.where(lane <= sub, size_rows, 0.0), axis=1, keepdims=True)
    ends = jnp.broadcast_to(ends, (128, 128))
    where_rows, window_rows, owner_rows, offset_rows = [], [], [], []
    for block in range(8):
        spot = position[pl.ds(block, 1), :]
        spots = jnp.broadcast_to(spot.astype(F32), (128, 128))
        past = spots >= ends
        owner = jnp.sum(jnp.where(past, 1.0, 0.0), axis=0, keepdims=True)
        begin = jnp.max(jnp.where(past, ends, 0.0), axis=0, keepdims=True)
        window = jnp.right_shift(spot, 7) - jnp.right_shift(begin.astype(jnp.int32), 7)
        owner_rows.append(owner)
        window_rows.append(window)
        where_rows.append(owner.astype(jnp.int32) * BUCKET + window)
        offset_rows.append(jnp.bitwise_and(spot, 127))
    offset_cols = jnp.concatenate(offset_rows, axis=0).astype(F32).T
    for block in range(8):
        rows = pl.ds(block * 128, 128)
        spread[rows, pl.ds(0, 128)] = vector[rows, :]
        spread[rows, pl.ds(128, 128)] = jnp.broadcast_to(
            offset_cols[:, block : block + 1], (128, 128)
        ).astype(BF16)

    part_sub = lax.broadcasted_iota(jnp.int32, (256, 128), 0)
    bucket_row = lax.broadcasted_iota(jnp.int32, (16, 16, 128), 1)
    bucket_lane = lax.broadcasted_iota(jnp.int32, (16, 16, 128), 2)
    for chunk in range(SLOTS // 256):
        picks = jnp.concatenate(
            [one_hot(part_sub + chunk * 256 == where_rows[block]) for block in range(8)], axis=1
        )
        both = jnp.dot(picks, spread[...], preferred_element_type=F32)
        data = both[:, :128].reshape(16, 16, 128)
        offsets = both[:, 128:].reshape(16, 16, 128)
        row = jnp.sum(
            jnp.where(bucket_row == bucket_lane, offsets, 0.0), axis=1, keepdims=True
        )
        data = jnp.where(bucket_row == 14, row, data)
        sent[pl.ds(chunk * 256, 256), :] = data.reshape(256, 128).astype(BF16)

    pl.semaphore_wait(barrier, LEAVES - 1)

    def bucket(index):
        return pl.ds(pl.multiple_of(index * BUCKET, BUCKET), BUCKET)

    for step in everyone:
        other = me ^ step
        pltpu.make_async_remote_copy(
            sent.at[bucket(other)],
            arrived.at[bucket(me)],
            send_sem.at[0],
            row_sem.at[0],
            device_id=other,
            device_id_type=LOGICAL,
        ).start()
    arrived[bucket(me), :] = sent[bucket(me), :]

    for copy in loads["right"]:
        copy.wait()

    @pl.loop(0, WINDOWS)
    def _(window):
        rows = pl.ds(pl.multiple_of(window * 128, 128), 128)
        for part in range(2):
            columns = pl.ds(pl.multiple_of(part * CAP + window * 128, 128), 128)
            for level in range(2):
                right_t[pl.ds(level * 128, 128), columns] = top_right[level, part, rows, :].T

    for copy in loads["left"]:
        copy.wait()

    @pl.loop(0, WINDOWS)
    def _(window):
        rows = pl.ds(pl.multiple_of(window * 128, 128), 128)
        for level in range(5):
            left[rows, pl.ds(512 + level * 128, 128)] = low_left[level, :, rows].T

    steps = jnp.bitwise_xor(lax.broadcasted_iota(jnp.int32, (1, 128), 1), me)
    places = jnp.full((1, 128), LEAVES - 1, jnp.int32)
    for place, step in enumerate(everyone):
        places = jnp.where(steps == step, place, places)
    places = jnp.broadcast_to(places.astype(F32), (128, 128)).T
    where_back = []
    for block in range(8):
        owners = jnp.broadcast_to(owner_rows[block], (128, 128)).astype(jnp.int32)
        place = jnp.sum(jnp.where(owners == sub, places, 0.0), axis=0, keepdims=True)
        where_back.append(place * BUCKET + window_rows[block].astype(F32))
    where_back = jnp.concatenate(where_back, axis=0).T
    for block in range(8):
        column = jnp.broadcast_to(where_back[:, block : block + 1], (128, 128)).astype(jnp.int32)
        for piece in range(SLOTS // 128):
            pick_t[pl.ds(block * 128, 128), pl.ds(piece * 128, 128)] = one_hot(
                column == lane + piece * 128
            )

    def landed(buffer, rows, semaphore):
        view = buffer.at[pl.ds(0, rows)]
        pltpu.make_async_copy(view, view, semaphore).wait()

    landed(arrived, SLOTS - BUCKET, row_sem.at[0])

    wide[...] = arrived[...].astype(F32)
    offsets = wide[pl.ds(14, 128, stride=16), :]
    offsets_t = offsets.T
    sub_f = sub.astype(F32)
    lane_f = lane.astype(F32)
    for window in range(WINDOWS):
        put = one_hot(jnp.broadcast_to(offsets_t[window : window + 1, :], (128, 128)) == sub_f)
        rows = wide[pl.ds(window, 128, stride=16), :].astype(BF16)
        values = jnp.dot(put, rows, preferred_element_type=F32)
        field[pl.ds(window * 128, 128), :] = values.astype(BF16)
        field[pl.ds(CAP + window * 128, 128), :] = rotated(values).astype(BF16)

    for levels in ((1, 2), (3, 4, 5, 6, 7)):
        span = pl.ds(START[levels[0]], sum(WIDTH[level] for level in levels))
        partial[span, :] = jnp.dot(right_t[span, :], field[...], preferred_element_type=F32)
        for level in levels:
            count, first, apart, rows = OWNERS[level]
            node = ((me >> (LEVELS - level)) ^ 1) << (LEVELS - level)
            place = me & (sources_of(level) - 1)
            index = (place & (sources_of(level) - 1)) // apart
            for step in far_first(range(count)):
                piece = index ^ step
                pltpu.make_async_remote_copy(
                    partial.at[pl.ds(pl.multiple_of(START[level] + piece * rows, 8), rows)],
                    sums[level].at[pl.ds(pl.multiple_of(place * rows, 8), rows)],
                    send_sem.at[1],
                    part_sem.at[level - 1],
                    device_id=node + first + piece * apart,
                    device_id_type=LOGICAL,
                ).start()

    for copy in loads["diag"]:
        copy.wait()

    @pl.loop(0, CAP // 256)
    def _(chunk):
        rows = pl.ds(pl.multiple_of(chunk * 256, 256), 256)
        result[rows, :] = jnp.dot(
            diag[0, rows, :], field[pl.ds(0, CAP), :], preferred_element_type=F32
        ) + jnp.dot(diag[1, rows, :], field[pl.ds(CAP, CAP), :], preferred_element_type=F32)

    for window in range(WINDOWS):
        column = jnp.broadcast_to(offsets[:, window : window + 1], (128, 128))
        rows = pl.ds(window * 128, 128)
        put_t[rows, pl.ds(window % 2 * 128, 128)] = one_hot(column == lane_f)
        put_t[rows, pl.ds(128 - window % 2 * 128, 128)] = jnp.zeros((128, 128), BF16)
    wide[pl.ds(14, 128, stride=16), :] = jnp.zeros((128, 128), F32)
    wide[pl.ds(15, 128, stride=16), :] = jnp.zeros((128, 128), F32)

    for level in range(6, 0, -1):
        count, first, apart, rows = OWNERS[level]
        place = me & (sources_of(level) - 1)

        @pl.when(place % apart == first)
        def _(level=level, rows=rows, index=place // apart):
            sources = sources_of(level)
            landed(sums[level], sources * rows, part_sem.at[level - 1])
            total = jnp.sum(sums[level][...].reshape(sources, rows, 128), axis=0)
            rank = ranks[(1 << level) - 2 + (me >> (LEVELS - level))]
            row = lax.broadcasted_iota(jnp.int32, (rows, 128), 0) + index * rows
            mine = pl.ds(pl.multiple_of(index * rows, rows), rows)
            got[level][mine, :] = jnp.where(row < rank, total, 0.0).astype(sum_type(level))
            for step in far_first(range(1, sources_of(level))):
                pltpu.make_async_remote_copy(
                    got[level].at[mine],
                    got[level].at[mine],
                    send_sem.at[2],
                    coef_sem.at[level - 1],
                    device_id=me ^ step,
                    device_id_type=LOGICAL,
                ).start()

    def set_coef(level, values):
        begin = START[level] * 2
        width = WIDTH[level]
        coef[pl.ds(begin, width), :] = values.astype(BF16)
        coef[pl.ds(begin + width, width), :] = rotated(values.astype(F32)).astype(BF16)

    landed(sums[7], 64, part_sem.at[6])
    row = lax.broadcasted_iota(jnp.int32, (64, 128), 0)
    set_coef(7, jnp.where(row < ranks[(1 << 7) - 2 + me], sums[7][...], 0.0).astype(BF16))

    def await_coef(level):
        count, first, apart, rows = OWNERS[level]
        owner = (me & (sources_of(level) - 1)) % apart == first

        @pl.when(owner)
        def _():
            landed(got[level], WIDTH[level] - rows, coef_sem.at[level - 1])

        if apart > 1:

            @pl.when(jnp.logical_not(owner))
            def _():
                landed(got[level], WIDTH[level], coef_sem.at[level - 1])

        set_coef(level, got[level][...])

    for level in range(6, 2, -1):
        await_coef(level)
    for chunk in range(CAP // 256):
        rows = pl.ds(chunk * 256, 256)
        result[rows, :] += jnp.dot(
            left[rows, pl.ds(512, 640)], coef[pl.ds(512, 640), :], preferred_element_type=F32
        )
    for level in (2, 1):
        await_coef(level)

    for chunk in range(CAP // 256):
        rows = pl.ds(chunk * 256, 256)
        values = result[rows, :] + jnp.dot(
            left[rows, pl.ds(0, 512)], coef[pl.ds(0, 512), :], preferred_element_type=F32
        )
        field[rows, :] = values.astype(BF16)
    for chunk in range(CAP // 256):
        rows = pl.ds(chunk * 256, 256)
        leaving = jnp.dot(put_t[rows, :], field[rows, :], preferred_element_type=F32)
        for half in range(2):
            wide[pl.ds(chunk * 2 + half, 128, stride=16), :] = leaving[half * 128 : half * 128 + 128]
    returning[...] = wide[...].astype(BF16)
    for place, step in enumerate(everyone):
        other = me ^ step
        pltpu.make_async_remote_copy(
            returning.at[bucket(other)],
            returned.at[pl.ds(place * BUCKET, BUCKET)],
            send_sem.at[3],
            row_sem.at[1 + turn_of(place)],
            device_id=other,
            device_id_type=LOGICAL,
        ).start()
    returned[pl.ds(SLOTS - BUCKET, BUCKET), :] = returning[bucket(me), :]

    landed(sent, SLOTS - BUCKET, send_sem.at[0])
    landed(partial, TOTAL, send_sem.at[1])
    for level in range(1, 7):
        count, first, apart, rows = OWNERS[level]

        @pl.when((me & (sources_of(level) - 1)) % apart == first)
        def _(level=level, rows=rows):
            landed(sent, (sources_of(level) - 1) * max(rows, 16), send_sem.at[2])

    for turn, (begin, end) in enumerate(zip(TURNS[:-1], TURNS[1:])):
        count = (end - begin) * BUCKET
        landed(returned, count - BUCKET if end == LEAVES else count, row_sem.at[1 + turn])
        span = pl.ds(begin * BUCKET, count)
        for chunk in range(ROWS // 256):
            rows = pl.ds(chunk * 256, 256)
            total = jnp.dot(pick_t[rows, span], returned[span, :], preferred_element_type=F32)
            if turn > 0:
                total += result[rows, :]
            if end < LEAVES:
                result[rows, :] = total
            else:
                product[rows, :] = total.astype(BF16)
    landed(returning, SLOTS - BUCKET, send_sem.at[3])


def on_device(
    mesh_vector,
    cluster_position,
    cluster_sizes,
    block_ranks,
    diag_block,
    top_left,
    top_right,
    low_left,
    low_right,
):
    scratch = [
        pltpu.SMEM((254,), jnp.int32),
        pltpu.VMEM((ROWS, 128), BF16),
        pltpu.VMEM((8, 128), jnp.int32),
        pltpu.VMEM((1, 128), jnp.int32),
        pltpu.VMEM((2, CAP, CAP), BF16),
        pltpu.VMEM((2, 2, CAP, 128), BF16),
        pltpu.VMEM((5, 128, CAP), BF16),
        pltpu.VMEM((TOTAL, 2 * CAP), BF16),
        pltpu.VMEM((CAP, 2 * TOTAL), BF16),
        pltpu.VMEM((ROWS, 256), BF16),
        pltpu.VMEM((ROWS, SLOTS), BF16),
        pltpu.VMEM((CAP, 256), BF16),
        pltpu.VMEM((SLOTS, 128), BF16),
        pltpu.VMEM((SLOTS, 128), BF16),
        pltpu.VMEM((SLOTS, 128), F32),
        pltpu.VMEM((2 * CAP, 128), BF16),
        pltpu.VMEM((TOTAL, 128), F32),
        pltpu.VMEM((CAP, 128), F32),
        pltpu.VMEM((2 * TOTAL, 128), BF16),
        pltpu.VMEM((SLOTS, 128), BF16),
        pltpu.VMEM((SLOTS, 128), BF16),
    ]
    scratch += [
        pltpu.VMEM(((1 << (LEVELS - level)) * OWNERS[level][3], 128), F32) for level in range(1, 8)
    ]
    scratch += [pltpu.VMEM((WIDTH[level], 128), sum_type(level)) for level in range(1, 7)]
    scratch += [
        pltpu.SemaphoreType.DMA((25,)),
        pltpu.SemaphoreType.DMA((4,)),
        pltpu.SemaphoreType.DMA((5,)),
        pltpu.SemaphoreType.DMA((7,)),
        pltpu.SemaphoreType.DMA((6,)),
    ]
    product = pl.pallas_call(
        body,
        out_shape=pltpu.VMEM((ROWS, 128), BF16),
        in_specs=[pl.BlockSpec(memory_space=pltpu.HBM)] * 9,
        out_specs=pl.BlockSpec(memory_space=pltpu.VMEM),
        scratch_shapes=scratch,
        compiler_params=pltpu.CompilerParams(
            collective_id=0, has_side_effects=True, vmem_limit_bytes=53 * 2**20
        ),
        name="tree_product",
    )(*(pltpu.with_memory_space_constraint(operand, pltpu.HBM) for operand in (
        block_ranks,
        mesh_vector,
        cluster_position.reshape(8, 128),
        cluster_sizes.reshape(1, 128),
        diag_block,
        top_left,
        top_right,
        jnp.swapaxes(low_left, 2, 3).reshape(5, 128, CAP),
        jnp.swapaxes(low_right, 2, 3),
    )))
    return product.astype(F32)


def solution(mesh):
    return jax.shard_map(
        on_device,
        mesh=mesh,
        in_specs=(
            P(("group", "member"), None),
            P(("group", "member")),
            P(),
            P(),
            P(None, ("group", "member"), None),
            P(None, None, ("group", "member"), None),
            P(None, None, ("group", "member"), None),
            P(None, None, ("group", "member"), None),
            P(None, None, ("group", "member"), None),
        ),
        out_specs=P(("group", "member"), None),
        check_vma=False,
    )
```

```python
import jax
import jax.numpy as jnp
from jax import lax
from jax.experimental import pallas as pl
from jax.experimental.pallas import tpu as pltpu
from jax.sharding import PartitionSpec as P

LOGICAL = pl.DeviceIdType.LOGICAL
F32 = jnp.float32
BF16 = jnp.bfloat16
LEAVES = 128
LEVELS = 7
ROWS = 1024
CAP = 1792
BUCKET = 16
WINDOWS = CAP // 128
SLOTS = LEAVES * BUCKET
WIDTH = {1: 128, 2: 128, 3: 64, 4: 64, 5: 64, 6: 64, 7: 64}
START = {1: 0, 2: 128, 3: 256, 4: 320, 5: 384, 6: 448, 7: 512}
TOTAL = 576
TURNS = (0, 32, 64, 96, 128)
OWNERS = {
    1: (16, 0, 4, 8),
    2: (8, 3, 4, 16),
    3: (4, 1, 4, 16),
    4: (4, 1, 2, 16),
    5: (4, 0, 1, 16),
    6: (2, 0, 1, 32),
    7: (1, 0, 1, 64),
}


def hops(step):
    ring = (0, 1, 2, 1)
    return ring[step >> 1 & 3] + ring[step >> 3 & 3] + ring[step >> 5 & 3]


def far_first(steps):
    return sorted(steps, key=lambda step: (-hops(step), -(step & 1)))


def sources_of(level):
    return 1 << (LEVELS - level)


def sum_type(level):
    return BF16 if OWNERS[level][3] >= 16 else F32


def turn_of(place):
    return sum(place >= begin for begin in TURNS[1:-1])


def rotated(values):
    lane = lax.broadcasted_iota(jnp.int32, values.shape, 1)
    turned = pltpu.roll(values, 64, 1)
    return jnp.where(lane < 64, -turned, turned)


def one_hot(mask):
    return jnp.where(mask, 1.0, 0.0).astype(BF16)


def body(
    ranks_hbm,
    vector_hbm,
    position_hbm,
    sizes_hbm,
    diag_hbm,
    top_left_hbm,
    top_right_hbm,
    low_left_hbm,
    low_right_hbm,
    product,
    ranks,
    vector,
    position,
    sizes,
    diag,
    top_right,
    low_left,
    right_t,
    left,
    spread,
    pick_t,
    put_t,
    sent,
    arrived,
    wide,
    field,
    partial,
    result,
    coef,
    returning,
    returned,
    *rest,
):
    sums = dict(zip(range(1, 8), rest[:7]))
    got = dict(zip(range(1, 7), rest[7:13]))
    load_sem, send_sem, row_sem, part_sem, coef_sem = rest[13:]
    me = lax.axis_index("group") * 32 + lax.axis_index("member")

    first_loads = [
        pltpu.make_async_copy(source, target, load_sem.at[21 + index])
        for index, (source, target) in enumerate(
            (
                (position_hbm, position),
                (sizes_hbm, sizes),
                (vector_hbm, vector),
                (ranks_hbm, ranks),
            )
        )
    ]
    for copy in first_loads:
        copy.start()
    barrier = pltpu.get_barrier_semaphore()
    everyone = far_first(range(1, LEAVES))
    for step in everyone:
        pl.semaphore_signal(barrier, inc=1, device_id=me ^ step, device_id_type=LOGICAL)

    loads = {
        "right": [
            pltpu.make_async_copy(top_right_hbm, top_right, load_sem.at[0]),
        ]
        + [
            pltpu.make_async_copy(
                low_right_hbm.at[level, part],
                right_t.at[pl.ds(256 + level * 64, 64), pl.ds(part * CAP, CAP)],
                load_sem.at[11 + level * 2 + part],
            )
            for level in range(5)
            for part in range(2)
        ],
        "left": [pltpu.make_async_copy(low_left_hbm, low_left, load_sem.at[2])]
        + [
            pltpu.make_async_copy(
                top_left_hbm.at[level, part],
                left.at[:, pl.ds((level * 2 + part) * 128, 128)],
                load_sem.at[3 + level * 2 + part],
            )
            for level in range(2)
            for part in range(2)
        ],
        "diag": [
            pltpu.make_async_copy(
                diag_hbm.at[part, pl.ds(half * 896, 896)],
                diag.at[part, pl.ds(half * 896, 896)],
                load_sem.at[7 + part * 2 + half],
            )
            for part in range(2)
            for half in range(2)
        ],
    }
    for name in ("right", "left", "diag"):
        for copy in loads[name]:
            copy.start()
    for copy in first_loads:
        copy.wait()

    sub = lax.broadcasted_iota(jnp.int32, (128, 128), 0)
    lane = lax.broadcasted_iota(jnp.int32, (128, 128), 1)
    size_rows = jnp.broadcast_to(sizes[...].astype(F32), (128, 128))
    ends = jnp.sum(jnp.where(lane <= sub, size_rows, 0.0), axis=1, keepdims=True)
    ends = jnp.broadcast_to(ends, (128, 128))
    where_rows, window_rows, owner_rows, offset_rows = [], [], [], []
    for block in range(8):
        spot = position[pl.ds(block, 1), :]
        spots = jnp.broadcast_to(spot.astype(F32), (128, 128))
        past = spots >= ends
        owner = jnp.sum(jnp.where(past, 1.0, 0.0), axis=0, keepdims=True)
        begin = jnp.max(jnp.where(past, ends, 0.0), axis=0, keepdims=True)
        window = jnp.right_shift(spot, 7) - jnp.right_shift(begin.astype(jnp.int32), 7)
        owner_rows.append(owner)
        window_rows.append(window)
        where_rows.append(owner.astype(jnp.int32) * BUCKET + window)
        offset_rows.append(jnp.bitwise_and(spot, 127))
    offset_cols = jnp.concatenate(offset_rows, axis=0).astype(F32).T
    for block in range(8):
        rows = pl.ds(block * 128, 128)
        spread[rows, pl.ds(0, 128)] = vector[rows, :]
        spread[rows, pl.ds(128, 128)] = jnp.broadcast_to(
            offset_cols[:, block : block + 1], (128, 128)
        ).astype(BF16)

    part_sub = lax.broadcasted_iota(jnp.int32, (256, 128), 0)
    bucket_row = lax.broadcasted_iota(jnp.int32, (16, 16, 128), 1)
    bucket_lane = lax.broadcasted_iota(jnp.int32, (16, 16, 128), 2)
    for chunk in range(SLOTS // 256):
        picks = jnp.concatenate(
            [one_hot(part_sub + chunk * 256 == where_rows[block]) for block in range(8)], axis=1
        )
        both = jnp.dot(picks, spread[...], preferred_element_type=F32)
        data = both[:, :128].reshape(16, 16, 128)
        offsets = both[:, 128:].reshape(16, 16, 128)
        row = jnp.sum(
            jnp.where(bucket_row == bucket_lane, offsets, 0.0), axis=1, keepdims=True
        )
        data = jnp.where(bucket_row == 14, row, data)
        sent[pl.ds(chunk * 256, 256), :] = data.reshape(256, 128).astype(BF16)

    pl.semaphore_wait(barrier, LEAVES - 1)

    def bucket(index):
        return pl.ds(pl.multiple_of(index * BUCKET, BUCKET), BUCKET)

    for step in everyone:
        other = me ^ step
        pltpu.make_async_remote_copy(
            sent.at[bucket(other)],
            arrived.at[bucket(me)],
            send_sem.at[0],
            row_sem.at[0],
            device_id=other,
            device_id_type=LOGICAL,
        ).start()
    arrived[bucket(me), :] = sent[bucket(me), :]

    for copy in loads["right"]:
        copy.wait()

    @pl.loop(0, WINDOWS)
    def _(window):
        rows = pl.ds(pl.multiple_of(window * 128, 128), 128)
        for part in range(2):
            columns = pl.ds(pl.multiple_of(part * CAP + window * 128, 128), 128)
            for level in range(2):
                right_t[pl.ds(level * 128, 128), columns] = top_right[level, part, rows, :].T

    for copy in loads["left"]:
        copy.wait()

    @pl.loop(0, WINDOWS)
    def _(window):
        rows = pl.ds(pl.multiple_of(window * 128, 128), 128)
        for level in range(5):
            left[rows, pl.ds(512 + level * 128, 128)] = low_left[level, :, rows].T

    steps = jnp.bitwise_xor(lax.broadcasted_iota(jnp.int32, (1, 128), 1), me)
    places = jnp.full((1, 128), LEAVES - 1, jnp.int32)
    for place, step in enumerate(everyone):
        places = jnp.where(steps == step, place, places)
    places = jnp.broadcast_to(places.astype(F32), (128, 128)).T
    where_back = []
    for block in range(8):
        owners = jnp.broadcast_to(owner_rows[block], (128, 128)).astype(jnp.int32)
        place = jnp.sum(jnp.where(owners == sub, places, 0.0), axis=0, keepdims=True)
        where_back.append(place * BUCKET + window_rows[block].astype(F32))
    where_back = jnp.concatenate(where_back, axis=0).T
    for block in range(8):
        column = jnp.broadcast_to(where_back[:, block : block + 1], (128, 128)).astype(jnp.int32)
        for piece in range(SLOTS // 128):
            pick_t[pl.ds(block * 128, 128), pl.ds(piece * 128, 128)] = one_hot(
                column == lane + piece * 128
            )

    def landed(buffer, rows, semaphore):
        view = buffer.at[pl.ds(0, rows)]
        pltpu.make_async_copy(view, view, semaphore).wait()

    landed(arrived, SLOTS - BUCKET, row_sem.at[0])

    wide[pl.ds(0, SLOTS), :] = arrived[...].astype(F32)
    offsets = wide[pl.ds(14, 128, stride=16), :]
    offsets_t = offsets.T
    sub_f = sub.astype(F32)
    lane_f = lane.astype(F32)
    for window in range(WINDOWS):
        put = one_hot(jnp.broadcast_to(offsets_t[window : window + 1, :], (128, 128)) == sub_f)
        rows = wide[pl.ds(window, 128, stride=16), :].astype(BF16)
        values = jnp.dot(put, rows, preferred_element_type=F32)
        field[pl.ds(window * 128, 128), :] = values.astype(BF16)
        field[pl.ds(CAP + window * 128, 128), :] = rotated(values).astype(BF16)

    for levels in ((1, 2), (3, 4, 5, 6, 7)):
        span = pl.ds(START[levels[0]], sum(WIDTH[level] for level in levels))
        partial[span, :] = jnp.dot(right_t[span, :], field[...], preferred_element_type=F32)
        for level in levels:
            count, first, apart, rows = OWNERS[level]
            node = ((me >> (LEVELS - level)) ^ 1) << (LEVELS - level)
            place = me & (sources_of(level) - 1)
            index = (place & (sources_of(level) - 1)) // apart
            for step in sorted(range(count), key=lambda step: -hops(sources_of(level) + step * apart)):
                piece = index ^ step
                pltpu.make_async_remote_copy(
                    partial.at[pl.ds(pl.multiple_of(START[level] + piece * rows, 8), rows)],
                    sums[level].at[pl.ds(pl.multiple_of(place * rows, 8), rows)],
                    send_sem.at[1],
                    part_sem.at[level - 1],
                    device_id=node + first + piece * apart,
                    device_id_type=LOGICAL,
                ).start()

    for copy in loads["diag"]:
        copy.wait()

    @pl.loop(0, CAP // 256)
    def _(chunk):
        rows = pl.ds(pl.multiple_of(chunk * 256, 256), 256)
        result[rows, :] = jnp.dot(
            diag[0, rows, :], field[pl.ds(0, CAP), :], preferred_element_type=F32
        ) + jnp.dot(diag[1, rows, :], field[pl.ds(CAP, CAP), :], preferred_element_type=F32)

    for window in range(WINDOWS):
        column = jnp.broadcast_to(offsets[:, window : window + 1], (128, 128))
        rows = pl.ds(window * 128, 128)
        put_t[rows, pl.ds(window % 2 * 128, 128)] = one_hot(column == lane_f)
        put_t[rows, pl.ds(128 - window % 2 * 128, 128)] = jnp.zeros((128, 128), BF16)
    wide[pl.ds(14, 128, stride=16), :] = jnp.zeros((128, 128), F32)
    wide[pl.ds(15, 128, stride=16), :] = jnp.zeros((128, 128), F32)

    for level in range(6, 0, -1):
        count, first, apart, rows = OWNERS[level]
        place = me & (sources_of(level) - 1)

        @pl.when(place % apart == first)
        def _(level=level, rows=rows, index=place // apart):
            sources = sources_of(level)
            landed(sums[level], sources * rows, part_sem.at[level - 1])
            total = jnp.sum(sums[level][...].reshape(sources, rows, 128), axis=0)
            rank = ranks[(1 << level) - 2 + (me >> (LEVELS - level))]
            row = lax.broadcasted_iota(jnp.int32, (rows, 128), 0) + index * rows
            mine = pl.ds(pl.multiple_of(index * rows, rows), rows)
            got[level][mine, :] = jnp.where(row < rank, total, 0.0).astype(sum_type(level))
            for step in far_first(range(1, sources_of(level))):
                pltpu.make_async_remote_copy(
                    got[level].at[mine],
                    got[level].at[mine],
                    send_sem.at[2],
                    coef_sem.at[level - 1],
                    device_id=me ^ step,
                    device_id_type=LOGICAL,
                ).start()

    def set_coef(level, values):
        begin = START[level] * 2
        width = WIDTH[level]
        coef[pl.ds(begin, width), :] = values.astype(BF16)
        coef[pl.ds(begin + width, width), :] = rotated(values.astype(F32)).astype(BF16)

    landed(sums[7], 64, part_sem.at[6])
    row = lax.broadcasted_iota(jnp.int32, (64, 128), 0)
    set_coef(7, jnp.where(row < ranks[(1 << 7) - 2 + me], sums[7][...], 0.0).astype(BF16))

    def await_coef(level):
        count, first, apart, rows = OWNERS[level]
        owner = (me & (sources_of(level) - 1)) % apart == first

        @pl.when(owner)
        def _():
            landed(got[level], WIDTH[level] - rows, coef_sem.at[level - 1])

        if apart > 1:

            @pl.when(jnp.logical_not(owner))
            def _():
                landed(got[level], WIDTH[level], coef_sem.at[level - 1])

        set_coef(level, got[level][...])

    for level in range(6, 2, -1):
        await_coef(level)
    for chunk in range(CAP // 256):
        rows = pl.ds(chunk * 256, 256)
        result[rows, :] += jnp.dot(
            left[rows, pl.ds(512, 640)], coef[pl.ds(512, 640), :], preferred_element_type=F32
        )
    for level in (2, 1):
        await_coef(level)

    for chunk in range(CAP // 256):
        rows = pl.ds(chunk * 256, 256)
        values = result[rows, :] + jnp.dot(
            left[rows, pl.ds(0, 512)], coef[pl.ds(0, 512), :], preferred_element_type=F32
        )
        field[rows, :] = values.astype(BF16)
    for chunk in range(CAP // 256):
        rows = pl.ds(chunk * 256, 256)
        leaving = jnp.dot(put_t[rows, :], field[rows, :], preferred_element_type=F32)
        for half in range(2):
            wide[pl.ds(chunk * 2 + half, 128, stride=16), :] = leaving[half * 128 : half * 128 + 128]
    returning[...] = wide[pl.ds(0, SLOTS), :].astype(BF16)
    for place, step in enumerate(everyone):
        other = me ^ step
        pltpu.make_async_remote_copy(
            returning.at[bucket(other)],
            returned.at[pl.ds(place * BUCKET, BUCKET)],
            send_sem.at[3],
            row_sem.at[1 + turn_of(place)],
            device_id=other,
            device_id_type=LOGICAL,
        ).start()
    returned[pl.ds(SLOTS - BUCKET, BUCKET), :] = returning[bucket(me), :]

    landed(sent, SLOTS - BUCKET, send_sem.at[0])
    landed(partial, TOTAL, send_sem.at[1])
    for level in range(1, 7):
        count, first, apart, rows = OWNERS[level]

        @pl.when((me & (sources_of(level) - 1)) % apart == first)
        def _(level=level, rows=rows):
            landed(sent, (sources_of(level) - 1) * max(rows, 16), send_sem.at[2])

    for turn, (begin, end) in enumerate(zip(TURNS[:-1], TURNS[1:])):
        count = (end - begin) * BUCKET
        landed(returned, count - BUCKET if end == LEAVES else count, row_sem.at[1 + turn])
        span = pl.ds(begin * BUCKET, count)
        for chunk in range(ROWS // 256):
            rows = pl.ds(chunk * 256, 256)
            total = jnp.dot(pick_t[rows, span], returned[span, :], preferred_element_type=F32)
            if turn > 0:
                total += result[rows, :]
            if end < LEAVES:
                result[rows, :] = total
            else:
                product[rows, :] = total.astype(BF16)
    landed(returning, SLOTS - BUCKET, send_sem.at[3])


def on_device(
    mesh_vector,
    cluster_position,
    cluster_sizes,
    block_ranks,
    diag_block,
    top_left,
    top_right,
    low_left,
    low_right,
):
    scratch = [
        pltpu.SMEM((254,), jnp.int32),
        pltpu.VMEM((ROWS, 128), BF16),
        pltpu.VMEM((8, 128), jnp.int32),
        pltpu.VMEM((1, 128), jnp.int32),
        pltpu.VMEM((2, CAP, CAP), BF16),
        pltpu.VMEM((2, 2, CAP, 128), BF16),
        pltpu.VMEM((5, 128, CAP), BF16),
        pltpu.VMEM((TOTAL, 2 * CAP), BF16),
        pltpu.VMEM((CAP, 2 * TOTAL), BF16),
        pltpu.VMEM((ROWS, 256), BF16),
        pltpu.VMEM((ROWS, SLOTS), BF16),
        pltpu.VMEM((CAP, 256), BF16),
        pltpu.VMEM((SLOTS, 128), BF16),
        pltpu.VMEM((SLOTS, 128), BF16),
        pltpu.VMEM((SLOTS + BUCKET, 128), F32),
        pltpu.VMEM((2 * CAP, 128), BF16),
        pltpu.VMEM((TOTAL, 128), F32),
        pltpu.VMEM((CAP, 128), F32),
        pltpu.VMEM((2 * TOTAL, 128), BF16),
        pltpu.VMEM((SLOTS, 128), BF16),
        pltpu.VMEM((SLOTS, 128), BF16),
    ]
    scratch += [
        pltpu.VMEM(((1 << (LEVELS - level)) * OWNERS[level][3], 128), F32) for level in range(1, 8)
    ]
    scratch += [pltpu.VMEM((WIDTH[level], 128), sum_type(level)) for level in range(1, 7)]
    scratch += [
        pltpu.SemaphoreType.DMA((25,)),
        pltpu.SemaphoreType.DMA((4,)),
        pltpu.SemaphoreType.DMA((5,)),
        pltpu.SemaphoreType.DMA((7,)),
        pltpu.SemaphoreType.DMA((6,)),
    ]
    product = pl.pallas_call(
        body,
        out_shape=pltpu.VMEM((ROWS, 128), BF16),
        in_specs=[pl.BlockSpec(memory_space=pltpu.HBM)] * 9,
        out_specs=pl.BlockSpec(memory_space=pltpu.VMEM),
        scratch_shapes=scratch,
        compiler_params=pltpu.CompilerParams(
            collective_id=0, has_side_effects=True, vmem_limit_bytes=53 * 2**20
        ),
        name="tree_product",
    )(*(pltpu.with_memory_space_constraint(operand, pltpu.HBM) for operand in (
        block_ranks,
        mesh_vector,
        cluster_position.reshape(8, 128),
        cluster_sizes.reshape(1, 128),
        diag_block,
        top_left,
        top_right,
        jnp.swapaxes(low_left, 2, 3).reshape(5, 128, CAP),
        jnp.swapaxes(low_right, 2, 3),
    )))
    return product.astype(F32)


def solution(mesh):
    return jax.shard_map(
        on_device,
        mesh=mesh,
        in_specs=(
            P(("group", "member"), None),
            P(("group", "member")),
            P(),
            P(),
            P(None, ("group", "member"), None),
            P(None, None, ("group", "member"), None),
            P(None, None, ("group", "member"), None),
            P(None, None, ("group", "member"), None),
            P(None, None, ("group", "member"), None),
        ),
        out_specs=P(("group", "member"), None),
        check_vma=False,
    )
```
